32 devices in a mesh: dom: 8 (over y, x, core), case: 4 (over z).
Axes of the slice: x: 2, y: 2, z: 4, core: 2. Of those that a mesh axis runs over, the one named last changes fastest.
Arguments:
- displacement: float32 [64, 6, 32768], P('case', None, 'dom'), may hold values from -6 to 6
- adjoint: float32 [64, 6, 32768], P('case', None, 'dom'), may hold values from -6 to 6
- stiffness_ref: float32 [24, 24], replicated, may hold values from -0.25 to 0.25
- element_scale: float32 [8192], P('dom'), may hold values from 0.5 to 4
- connectivity: int32 [4, 8192], P(None, 'dom'), may hold values from 0 to 5119
- shared_nodes: int32 [2, 4096], P(None, 'dom'), may hold values from 0 to 4095
- spline_node: int32 [64, 128], P('dom'), may hold values from 0 to 4095
- spline_panel: int32 [64, 128], P('dom'), may hold values from 0 to 63
- spline_weight: float32 [64, 128], P('dom'), may hold values from -2 to 2
- spline_count: int32 [64], P('dom'), may hold values from 1 to 128, as said below
- case_weight: float32 [64], P('case'), may hold values from 0.3 to 3
Outputs:
- thickness_grad: float32 [8192], P(('dom', 'case'))
- panel_grad: float32 [512], P(('dom', 'case'))
The draws below stay inside these ranges and needn't reach their ends.
Inputs may be any that keep to these rules, and one draw needn't show every extreme that they name: `spline_count`: in each partition's 8 entries some entry equals 128.
All inputs are finite; a program needn't handle non-finite values.
Results may differ from the reference program's by a relative error of at most 0.0003.
Values sent between devices are 32-bit elements; how exact they have to be, the bound alone decides.
A program may use at most 128 MiB of HBM per device.

```python
import math
import jax
import jax.numpy as jnp
from jax import lax

NODES_DEV = 4096
ELEM_DEV = 1024
SHARED = 512
PANELS_DEV = 64
SLOTS = 128
DOF = 6
CORNERS = 4
NODES = 32768
ELEMS = 8192
CASES = 64
LINKS = 64
N_DOM = 8


def draw_spline_count(key, part):
    key = jax.random.fold_in(key, 7)
    key_heavy, key_full, key_light, key_chosen = jax.random.split(key, 4)
    heavy_peer = jax.random.randint(key_heavy, (1, N_DOM), 0, 4) == 0
    full_counts = jax.random.randint(key_full, (N_DOM, N_DOM), 1, SLOTS + 1)
    light_counts = jax.random.randint(key_light, (N_DOM, N_DOM), 1, SLOTS // 4 + 1)
    counts = jnp.where(heavy_peer, full_counts, light_counts)
    chosen_peer = jax.random.randint(key_chosen, (N_DOM, 1), 0, N_DOM)
    columns = jnp.arange(N_DOM, dtype=jnp.int32)[None, :]
    counts = jnp.where(columns == chosen_peer, SLOTS, counts)
    return counts.reshape(N_DOM * N_DOM).astype(jnp.int32)


def with_ends(values, stream_key, least, high):
    longest = values.shape.index(max(values.shape))
    spots = []
    for shift in (0, 1):
        where = [jax.random.randint(jax.random.fold_in(stream_key, axis), (), 0, length) for axis, length in enumerate(values.shape)]
        where[longest] = (where[longest] + shift) % values.shape[longest]
        spots.append(tuple(where))
    return values.at[spots[0]].set(least).at[spots[1]].set(high)


def block_scale(stream_key, shape, pieces, smallest, largest):
    def one(dim, shards_of):
        heights = jax.random.uniform(jax.random.fold_in(jax.random.fold_in(stream_key, 6), dim), (shards_of,), jnp.float32, smallest / len(pieces), largest / len(pieces))
        return jnp.repeat(jnp.exp(heights), shape[dim] // shards_of).reshape((-1,) + (1,) * (len(shape) - dim - 1))

    factor_of = one(*pieces[0])
    for cut in pieces[1:]:
        factor_of = factor_of * one(*cut)
    return factor_of


def bell_draw(stream_key, shape, scale, reach, pieces=(), kind=jnp.bfloat16):
    drawn = jax.random.normal(stream_key, shape, jnp.float32) * scale
    if len(pieces) > 0:
        drawn = block_scale(stream_key, shape, pieces, -0.22, 0.18) * drawn
    return jnp.clip(drawn, min=-reach, max=reach).astype(kind)


def setup_inputs(seed: int = 0) -> dict:
    key_of = jax.random.split(jax.random.key(seed), 12)
    return {
        "displacement": bell_draw(key_of[0], (CASES, DOF, NODES), 1.0, 6.0, ((0, 4), (2, 8)), jnp.float32),
        "adjoint": bell_draw(key_of[1], (CASES, DOF, NODES), 1.0, 6.0, ((0, 4), (2, 8)), jnp.float32),
        "stiffness_ref": bell_draw(key_of[2], (DOF * CORNERS, DOF * CORNERS), (DOF * CORNERS * DOF * CORNERS) ** -0.5, 0.25, (), jnp.float32),
        "element_scale": jnp.clip(jnp.exp(math.log(4.0) - 2.0794415 * jax.random.uniform(key_of[3], (ELEMS,), jnp.float32) ** block_scale(key_of[3], (ELEMS,), ((0, 8),), -0.2, 0.2)), 0.5, 4.0),
        "connectivity": with_ends(jax.random.randint(key_of[4], (CORNERS, ELEMS), 0, NODES_DEV + 2 * SHARED), jax.random.fold_in(key_of[4], 1), 0, (NODES_DEV + 2 * SHARED) - 1).astype(jnp.int32),
        "shared_nodes": with_ends(jax.random.randint(key_of[5], (2, SHARED * N_DOM), 0, NODES_DEV), jax.random.fold_in(key_of[5], 1), 0, NODES_DEV - 1).astype(jnp.int32),
        "spline_node": with_ends(jax.random.randint(key_of[6], (LINKS, SLOTS), 0, NODES_DEV), jax.random.fold_in(key_of[6], 1), 0, NODES_DEV - 1).astype(jnp.int32),
        "spline_panel": with_ends(jax.random.randint(key_of[7], (LINKS, SLOTS), 0, PANELS_DEV), jax.random.fold_in(key_of[7], 1), 0, PANELS_DEV - 1).astype(jnp.int32),
        "spline_weight": bell_draw(key_of[8], (LINKS, SLOTS), (N_DOM * SLOTS // (2 * PANELS_DEV)) ** -0.5, 2.0, ((0, 8),), jnp.float32),
        "spline_count": draw_spline_count(jax.random.fold_in(key_of[11], 71), 0),
        "case_weight": jnp.clip(jnp.exp(math.log(3.0) - 2.3025851 * jax.random.uniform(key_of[10], (CASES,), jnp.float32) ** block_scale(key_of[10], (CASES,), ((0, 4),), -0.2, 0.2)), 0.3, 3.0),
    }


def reference(displacement, adjoint, stiffness_ref, element_scale, connectivity, shared_nodes, spline_node, spline_panel, spline_weight, spline_count, case_weight):
    case_count = displacement.shape[0]
    width = stiffness_ref.shape[0]

    def ghosts(source, part_index, row):
        own_block = lax.dynamic_slice_in_dim(source, part_index * NODES_DEV, NODES_DEV, 2)
        chosen = lax.dynamic_slice_in_dim(shared_nodes[row], part_index * SHARED, SHARED, 0)
        return own_block[:, :, chosen]

    def one_part(part_index):
        lower_part = jnp.clip(part_index - 1, 0, N_DOM - 1).astype(jnp.int32)
        upper_part = jnp.clip(part_index + 1, 0, N_DOM - 1).astype(jnp.int32)
        corners = lax.dynamic_slice_in_dim(connectivity, part_index * ELEM_DEV, ELEM_DEV, 1)
        fields = []
        for source in (displacement, adjoint):
            own_block = lax.dynamic_slice_in_dim(source, part_index * NODES_DEV, NODES_DEV, 2)
            from_lower = jnp.where(part_index > 0, ghosts(source, lower_part, 1), 0.0)
            from_upper = jnp.where(part_index < N_DOM - 1, ghosts(source, upper_part, 0), 0.0)
            extended = jnp.concatenate([own_block, from_lower, from_upper], axis=2)
            fields.append(extended[:, :, corners].reshape(case_count, width, ELEM_DEV))
        stiffness = jnp.einsum('ab,cbe->cae', stiffness_ref, fields[0], precision=lax.Precision.HIGHEST)
        energy = lax.optimization_barrier(jnp.sum(fields[1] * stiffness, axis=1))
        scaling = lax.dynamic_slice_in_dim(element_scale, part_index * ELEM_DEV, ELEM_DEV, 0)
        return -scaling * jnp.dot(case_weight, energy, precision=lax.Precision.HIGHEST) / math.sqrt(case_count)
    thickness_grad = lax.map(one_part, jnp.arange(N_DOM, dtype=jnp.int32)).reshape(-1)
    row_count = N_DOM * N_DOM
    row_ids = jnp.arange(row_count, dtype=jnp.int32)
    source_part = row_ids // N_DOM
    destination = row_ids % N_DOM
    global_node = (source_part[:, None] * NODES_DEV + spline_node).reshape(-1)
    live_slot = jnp.arange(SLOTS, dtype=jnp.int32)[None, :] < spline_count[:, None]
    coefficient = jnp.where(live_slot, spline_weight, 0.0).reshape(-1)
    target_panel = (destination[:, None] * PANELS_DEV + spline_panel).reshape(-1)

    def normal_wash(source):
        values = source[:, 2, :][:, global_node] * coefficient[None, :]
        return jax.ops.segment_sum(values.T, target_panel, num_segments=N_DOM * PANELS_DEV).T
    product = normal_wash(displacement) * normal_wash(adjoint)
    panel_grad = jnp.dot(case_weight, product, precision=lax.Precision.HIGHEST) / math.sqrt(case_count)
    return (thickness_grad, panel_grad)
```

```python
import functools
import math

import jax
import jax.numpy as jnp
from jax import lax
from jax.experimental import pallas as pl
from jax.experimental.pallas import tpu as pltpu
from jax.sharding import PartitionSpec as P

PANELS_DEV = 64
LANES = 128
HIGHEST = lax.Precision.HIGHEST
MESH = pl.DeviceIdType.MESH
PACK = (0, 16, 64, 80)


def iota(shape, dim):
    return lax.broadcasted_iota(jnp.int32, shape, dim)


def dot_lanes(a, b):
    return lax.dot_general(
        a, b, (((1,), (1,)), ((), ())), precision=HIGHEST, preferred_element_type=jnp.float32
    )


def kernel(
    n_dom,
    groups,
    u_ref,
    a_ref,
    k_ref,
    scale_ref,
    panel_ref,
    weight_ref,
    conn_ref,
    shared_ref,
    node_ref,
    count_ref,
    case_ref,
    thick_ref,
    wash_ref,
    table,
    picked,
    halo_pick,
    halo_out,
    halo_in,
    spline_pick,
    spline_out,
    spline_in,
    big_hi,
    big_lo,
    thick,
    message,
    arrived,
    halo_send,
    halo_recv,
    spline_send,
    spline_recv,
    case_send,
    case_recv,
):
    cases = case_ref.shape[0]
    nodes = u_ref.shape[1]
    corners, elements = conn_ref.shape
    shared = shared_ref.shape[1]
    slots = node_ref.shape[1]
    half = shared // 2
    share_rows = elements // LANES // groups
    dom, case = lax.axis_index("dom"), lax.axis_index("case")

    barrier = pltpu.get_barrier_semaphore()
    for off in range(1, n_dom):
        pl.semaphore_signal(
            barrier, inc=1, device_id=(lax.rem(dom + off, n_dom), case), device_id_type=MESH
        )
    for off in range(1, groups):
        pl.semaphore_signal(
            barrier, inc=1, device_id=(dom, lax.rem(case + off, groups)), device_id_type=MESH
        )

    rest = u_ref.shape[0] - 32

    def turn(block, carry):
        cols = pl.ds(pl.multiple_of(block * LANES, LANES), LANES)
        first = jnp.concatenate([u_ref[:, cols], a_ref[0:32, cols]], axis=0)
        second = jnp.concatenate(
            [a_ref[32 : 32 + rest, cols], jnp.zeros((LANES - rest, LANES), jnp.float32)], axis=0
        )
        start = pl.multiple_of(block * 2 * LANES, 2 * LANES)
        table[pl.ds(start, LANES, stride=2), :] = first.T
        table[pl.ds(start + 1, LANES, stride=2), :] = second.T
        return carry

    lax.fori_loop(0, nodes // LANES, turn, 0, unroll=2)

    lane = iota((1, LANES), 1)
    low_half = lane < 64

    def pick_halo(side):
        def step(i, carry):
            for t in range(16):
                n = i * 16 + t
                halo_pick[side, pl.ds(2 * n, 2), :] = table[
                    pl.ds(2 * shared_ref[side, n], 2), :
                ]
            return carry

        lax.fori_loop(0, shared // 16, step, 0)
        halo_out[side, 0:shared, :] = halo_pick[side, pl.ds(0, shared, stride=2), :]
        halo_out[side, shared : shared + half, :] = halo_pick[
            side, pl.ds(1, half, stride=2), :
        ] + pltpu.roll(halo_pick[side, pl.ds(shared + 1, half, stride=2), :], 64, 1)

    def halo_copy(side):
        other = dom - 1 if side == 0 else dom + 1
        return pltpu.make_async_remote_copy(
            src_ref=halo_out.at[side],
            dst_ref=halo_in.at[1 - side],
            send_sem=halo_send.at[side],
            recv_sem=halo_recv.at[1 - side],
            device_id=(other, case),
            device_id_type=MESH,
        )

    pick_halo(0)
    pl.semaphore_wait(barrier, n_dom - 1 + groups - 1)

    @pl.when(dom > 0)
    def _():
        halo_copy(0).start()

    pick_halo(1)

    @pl.when(dom < n_dom - 1)
    def _():
        halo_copy(1).start()

    def pick_spline(i, carry):
        row = i // (slots // 16)
        col = (i % (slots // 16)) * 16
        for t in range(16):
            spline_pick[pl.ds(2 * (i * 16 + t), 2), :] = table[
                pl.ds(2 * node_ref[row, col + t], 2), :
            ]
        return carry

    lax.fori_loop(0, n_dom * slots // 16, pick_spline, 0)
    is_u = (lane >= 32) & (lane < 48)
    is_a = lane < 16

    def spline_block(j, carry):
        base = pl.multiple_of(j * 2 * slots, 2 * slots)
        first = spline_pick[pl.ds(base, slots, stride=2), :]
        second = spline_pick[pl.ds(base + 1, slots, stride=2), :]
        values = jnp.where(is_u, first, jnp.where(is_a, second, 0.0))
        coefficient = jnp.where(
            iota((1, slots), 1) < count_ref[j], weight_ref[pl.ds(j, 1), :], 0.0
        )
        onehot = jnp.where(
            iota((PANELS_DEV, slots), 0) == panel_ref[pl.ds(j, 1), :], coefficient, 0.0
        )
        wash = jnp.dot(onehot, values, precision=HIGHEST, preferred_element_type=jnp.float32)
        packed = wash[0:16]
        for g in range(1, 4):
            packed = packed + pltpu.roll(wash[16 * g : 16 * g + 16], PACK[g], 1)
        spline_out[j] = packed
        return carry

    lax.fori_loop(0, n_dom, spline_block, 0)

    def spline_copy(off):
        other = lax.rem(dom + off, n_dom)
        return pltpu.make_async_remote_copy(
            src_ref=spline_out.at[other],
            dst_ref=spline_in.at[dom],
            send_sem=spline_send.at[off],
            recv_sem=spline_recv.at[off],
            device_id=(other, case),
            device_id_type=MESH,
        )

    for off in range(1, n_dom):
        spline_copy(off).start()

    width = corners * LANES
    wide = k_ref.shape[0]
    weights = jnp.zeros((1, width), jnp.float32)
    wide_lane = iota((1, width), 1)
    for c in range(cases):
        weights = jnp.where(wide_lane % 16 == c, case_ref[c], weights)
    r = iota((width, wide), 0)
    u_dof = (r % LANES) // 16
    to_u = jnp.where(iota((width, wide), 1) == u_dof * 4 + r // LANES, 1.0, 0.0)
    q = iota((wide, width), 1)
    a_dof = ((q % LANES) // 16 + 2) % 8
    to_a = jnp.where(iota((wide, width), 0) == a_dof * 4 + q // LANES, 1.0, 0.0)
    big = jnp.dot(
        dot_lanes(to_u, k_ref[...]), to_a, precision=HIGHEST, preferred_element_type=jnp.float32
    )
    same_case = iota((width, width), 0) % 16 == iota((width, width), 1) % 16
    big = jnp.where(same_case, big * weights, 0.0)
    hi = big.astype(jnp.bfloat16)
    big_hi[...] = hi
    big_lo[...] = (big - hi.astype(jnp.float32)).astype(jnp.bfloat16)

    def unpack(side):
        base = 2 * (nodes + side * shared)
        table[pl.ds(base, shared, stride=2), :] = halo_in[side, 0:shared, :]
        both = halo_in[side, shared : shared + half, :]
        table[pl.ds(base + 1, half, stride=2), :] = jnp.where(low_half, both, 0.0)
        table[pl.ds(base + shared + 1, half, stride=2), :] = jnp.where(
            low_half, pltpu.roll(both, 64, 1), 0.0
        )

    def blank(side):
        base = 2 * (nodes + side * shared)
        table[base : base + 2 * shared, :] = jnp.zeros((2 * shared, LANES), jnp.float32)

    @pl.when(dom > 0)
    def _():
        halo_copy(1).wait_recv()
        unpack(0)

    @pl.when(dom == 0)
    def _():
        blank(0)

    @pl.when(dom < n_dom - 1)
    def _():
        halo_copy(0).wait_recv()
        unpack(1)

    @pl.when(dom == n_dom - 1)
    def _():
        blank(1)

    def pick_elements(i, carry):
        for t in range(8):
            for k in range(corners):
                e = i * 8 + t
                picked[k, pl.ds(2 * e, 2), :] = table[pl.ds(2 * conn_ref[k, e], 2), :]
        return carry

    lax.fori_loop(0, elements // 8, pick_elements, 0)
    ones = jnp.ones((8, LANES), jnp.float32)
    from_first = lane >= 96

    def energy_block(b, carry):
        base = pl.multiple_of(b * 2 * LANES, 2 * LANES)
        firsts = [picked[k, pl.ds(base, LANES, stride=2), :] for k in range(corners)]
        seconds = [picked[k, pl.ds(base + 1, LANES, stride=2), :] for k in range(corners)]
        u = jnp.concatenate(firsts, axis=1)
        u_hi = u.astype(jnp.bfloat16)
        u_lo = (u - u_hi.astype(jnp.float32)).astype(jnp.bfloat16)
        force = jnp.dot(u_hi, big_hi[...], preferred_element_type=jnp.float32)
        force = force + jnp.dot(u_lo, big_hi[...], preferred_element_type=jnp.float32)
        force = force + jnp.dot(u_hi, big_lo[...], preferred_element_type=jnp.float32)
        total = jnp.zeros((LANES, LANES), jnp.float32)
        for k in range(corners):
            adjoint = jnp.where(from_first, firsts[k], seconds[k])
            total = total + adjoint * force[:, k * LANES : (k + 1) * LANES]
        thick[pl.ds(b, 1), :] = dot_lanes(ones, total)[0:1]
        return carry

    lax.fori_loop(0, elements // LANES, energy_block, 0)

    spline_in[dom] = spline_out[dom]
    for off in range(1, n_dom):
        spline_copy(off).wait_recv()
    wash = spline_in[0]
    for s in range(1, n_dom):
        wash = wash + spline_in[s]
    product = wash * pltpu.roll(wash, LANES - 32, 1)
    spread = jnp.concatenate(
        [
            jnp.where((lane >= PACK[g]) & (lane < PACK[g] + 16), product, 0.0)
            for g in range(4)
        ],
        axis=0,
    )
    panels = dot_lanes(jnp.broadcast_to(weights[:, 0:LANES], (8, LANES)), spread)[0:1]

    message[...] = jnp.zeros_like(message)
    for z in range(groups):
        message[z, 0:share_rows, :] = thick[z * share_rows : (z + 1) * share_rows, :]
        message[z, share_rows : share_rows + 1, 0:PANELS_DEV] = panels

    def case_copy(off):
        other = lax.rem(case + off, groups)
        return pltpu.make_async_remote_copy(
            src_ref=message.at[other],
            dst_ref=arrived.at[case],
            send_sem=case_send.at[off],
            recv_sem=case_recv.at[off],
            device_id=(dom, other),
            device_id_type=MESH,
        )

    for off in range(1, groups):
        case_copy(off).start()
    arrived[case] = message[case]
    for off in range(1, groups):
        case_copy(off).wait_recv()
    total = arrived[0]
    for z in range(1, groups):
        total = total + arrived[z]
    root = math.sqrt(cases * groups)
    scaling = scale_ref[pl.ds(case * share_rows, share_rows), :]
    thick_ref[...] = -scaling * total[0:share_rows] / root
    panel_share = PANELS_DEV // groups
    shift = lax.rem(LANES - case * panel_share, LANES)
    wash_ref[...] = pltpu.roll(total, shift, 1)[share_rows : share_rows + 1] / root

    @pl.when(dom > 0)
    def _():
        halo_copy(0).wait_send()

    @pl.when(dom < n_dom - 1)
    def _():
        halo_copy(1).wait_send()

    for off in range(1, n_dom):
        spline_copy(off).wait_send()
    for off in range(1, groups):
        case_copy(off).wait_send()


def on_device(
    n_dom,
    groups,
    displacement,
    adjoint,
    stiffness_ref,
    element_scale,
    connectivity,
    shared_nodes,
    spline_node,
    spline_panel,
    spline_weight,
    spline_count,
    case_weight,
):
    cases, dof, nodes = displacement.shape
    corners, elements = connectivity.shape
    shared = shared_nodes.shape[1]
    slots = spline_node.shape[1]
    width = corners * LANES
    share_rows = elements // LANES // groups
    packed = shared + shared // 2
    f32 = jnp.float32
    vmem = pl.BlockSpec(memory_space=pltpu.VMEM)
    smem = pl.BlockSpec(memory_space=pltpu.SMEM)
    thick, panel = pl.pallas_call(
        functools.partial(kernel, n_dom, groups),
        out_shape=(
            jax.ShapeDtypeStruct((share_rows, LANES), f32),
            jax.ShapeDtypeStruct((1, LANES), f32),
        ),
        in_specs=[vmem] * 6 + [smem] * 5,
        out_specs=(vmem, vmem),
        scratch_shapes=[
            pltpu.VMEM((2 * (nodes + 2 * shared), LANES), f32),
            pltpu.VMEM((corners, 2 * elements, LANES), f32),
            pltpu.VMEM((2, 2 * shared, LANES), f32),
            pltpu.VMEM((2, packed, LANES), f32),
            pltpu.VMEM((2, packed, LANES), f32),
            pltpu.VMEM((2 * n_dom * slots, LANES), f32),
            pltpu.VMEM((n_dom, 16, LANES), f32),
            pltpu.VMEM((n_dom, 16, LANES), f32),
            pltpu.VMEM((width, width), jnp.bfloat16),
            pltpu.VMEM((width, width), jnp.bfloat16),
            pltpu.VMEM((elements // LANES, LANES), f32),
            pltpu.VMEM((groups, 8, LANES), f32),
            pltpu.VMEM((groups, 8, LANES), f32),
            pltpu.SemaphoreType.DMA((2,)),
            pltpu.SemaphoreType.DMA((2,)),
            pltpu.SemaphoreType.DMA((n_dom,)),
            pltpu.SemaphoreType.DMA((n_dom,)),
            pltpu.SemaphoreType.DMA((groups,)),
            pltpu.SemaphoreType.DMA((groups,)),
        ],
        compiler_params=pltpu.CompilerParams(
            collective_id=0, has_side_effects=True, vmem_limit_bytes=48 * 2**20
        ),
    )(
        jnp.transpose(displacement, (1, 0, 2)).reshape(dof * cases, nodes),
        jnp.transpose(adjoint, (1, 0, 2)).reshape(dof * cases, nodes),
        stiffness_ref,
        element_scale.reshape(elements // LANES, LANES),
        spline_panel,
        spline_weight,
        connectivity,
        shared_nodes,
        spline_node,
        spline_count,
        case_weight,
    )
    return thick.reshape(share_rows * LANES), panel[0, : PANELS_DEV // groups]


def solution(mesh):
    return jax.shard_map(
        functools.partial(on_device, mesh.shape["dom"], mesh.shape["case"]),
        mesh=mesh,
        in_specs=(
            P("case", None, "dom"),
            P("case", None, "dom"),
            P(),
            P("dom"),
            P(None, "dom"),
            P(None, "dom"),
            P("dom", None),
            P("dom", None),
            P("dom", None),
            P("dom"),
            P("case"),
        ),
        out_specs=(P(("dom", "case")), P(("dom", "case"))),
        check_vma=False,
    )
```

```python
import functools
import math

import jax
import jax.numpy as jnp
from jax import lax
from jax.experimental import pallas as pl
from jax.experimental.pallas import tpu as pltpu
from jax.sharding import PartitionSpec as P

PANELS_DEV = 64
LANES = 128
HIGHEST = lax.Precision.HIGHEST
MESH = pl.DeviceIdType.MESH
PACK = (0, 16, 64, 80)
LOADS = 4


def iota(shape, dim):
    return lax.broadcasted_iota(jnp.int32, shape, dim)


def dot_lanes(a, b):
    return lax.dot_general(
        a, b, (((1,), (1,)), ((), ())), precision=HIGHEST, preferred_element_type=jnp.float32
    )


def kernel(
    n_dom,
    groups,
    u_hbm,
    a_hbm,
    *refs,
):
    smalls, refs = refs[:9], refs[9:]
    (thick_ref, wash_ref, u_ref, a_ref), refs = refs[:4], refs[4:]
    held, refs = refs[:9], refs[9:]
    (
        k_ref,
        scale_ref,
        panel_ref,
        weight_ref,
        conn_ref,
        shared_ref,
        node_ref,
        count_ref,
        case_ref,
    ) = held
    (
        table,
        picked,
        halo_pick,
        halo_out,
        halo_in,
        spline_pick,
        spline_out,
        spline_in,
        big_hi,
        big_lo,
        thick,
        message,
        arrived,
        halo_send,
        halo_recv,
        spline_send,
        spline_recv,
        case_send,
        case_recv,
        load_sem,
        small_sem,
    ) = refs
    cases = case_ref.shape[0]
    nodes = u_ref.shape[1]
    corners, elements = smalls[4].shape
    shared = smalls[5].shape[1]
    slots = smalls[6].shape[1]
    half = shared // 2
    share_rows = elements // LANES // groups
    dom, case = lax.axis_index("dom"), lax.axis_index("case")

    loads = []
    for part in range(LOADS):
        cols = pl.ds(part * (nodes // LOADS), nodes // LOADS)
        pair = [
            pltpu.make_async_copy(
                source.at[:, cols], target.at[:, cols], load_sem.at[which, part]
            )
            for which, (source, target) in enumerate(((u_hbm, u_ref), (a_hbm, a_ref)))
        ]
        for copy in pair:
            copy.start()
        loads.append(pair)
    small_pairs = []
    for source, target in zip(smalls, held):
        if source.shape == target.shape:
            small_pairs.append((source, target))
        else:
            size = source.shape[1]
            for row in range(source.shape[0]):
                small_pairs.append((source.at[row], target.at[pl.ds(row * size, size)]))
    small_loads = [
        pltpu.make_async_copy(source, target, small_sem.at[i])
        for i, (source, target) in enumerate(small_pairs)
    ]
    for copy in small_loads:
        copy.start()

    barrier = pltpu.get_barrier_semaphore()
    for off in range(1, n_dom):
        pl.semaphore_signal(
            barrier, inc=1, device_id=(lax.rem(dom + off, n_dom), case), device_id_type=MESH
        )
    for off in range(1, groups):
        pl.semaphore_signal(
            barrier, inc=1, device_id=(dom, lax.rem(case + off, groups)), device_id_type=MESH
        )

    rest = u_ref.shape[0] - 32

    def turn(block, carry):
        cols = pl.ds(pl.multiple_of(block * LANES, LANES), LANES)
        first = jnp.concatenate([u_ref[:, cols], a_ref[0:32, cols]], axis=0)
        second = jnp.concatenate(
            [a_ref[32 : 32 + rest, cols], jnp.zeros((LANES - rest, LANES), jnp.float32)], axis=0
        )
        start = pl.multiple_of(block * 2 * LANES, 2 * LANES)
        table[pl.ds(start, LANES, stride=2), :] = first.T
        table[pl.ds(start + 1, LANES, stride=2), :] = second.T
        return carry

    per_load = nodes // LANES // LOADS
    for part, pair in enumerate(loads):
        for copy in pair:
            copy.wait()
        lax.fori_loop(part * per_load, (part + 1) * per_load, turn, 0, unroll=8)
    for copy in small_loads:
        copy.wait()

    lane = iota((1, LANES), 1)
    low_half = lane < 64

    def pick_halo(side):
        def step(i, carry):
            for t in range(16):
                n = i * 16 + t
                halo_pick[side, pl.ds(2 * n, 2), :] = table[
                    pl.ds(2 * shared_ref[side * shared + n], 2), :
                ]
            return carry

        lax.fori_loop(0, shared // 16, step, 0)
        halo_out[side, 0:shared, :] = halo_pick[side, pl.ds(0, shared, stride=2), :]
        halo_out[side, shared : shared + half, :] = halo_pick[
            side, pl.ds(1, half, stride=2), :
        ] + pltpu.roll(halo_pick[side, pl.ds(shared + 1, half, stride=2), :], 64, 1)

    def halo_copy(side):
        other = dom - 1 if side == 0 else dom + 1
        return pltpu.make_async_remote_copy(
            src_ref=halo_out.at[side],
            dst_ref=halo_in.at[1 - side],
            send_sem=halo_send.at[side],
            recv_sem=halo_recv.at[1 - side],
            device_id=(other, case),
            device_id_type=MESH,
        )

    pick_halo(0)
    pl.semaphore_wait(barrier, n_dom - 1 + groups - 1)

    @pl.when(dom > 0)
    def _():
        halo_copy(0).start()

    pick_halo(1)

    @pl.when(dom < n_dom - 1)
    def _():
        halo_copy(1).start()

    def pick_spline(i, carry):
        for t in range(16):
            spline_pick[pl.ds(2 * (i * 16 + t), 2), :] = table[
                pl.ds(2 * node_ref[i * 16 + t], 2), :
            ]
        return carry

    lax.fori_loop(0, n_dom * slots // 16, pick_spline, 0)
    is_u = (lane >= 32) & (lane < 48)
    is_a = lane < 16

    def spline_block(j, carry):
        base = pl.multiple_of(j * 2 * slots, 2 * slots)
        first = spline_pick[pl.ds(base, slots, stride=2), :]
        second = spline_pick[pl.ds(base + 1, slots, stride=2), :]
        values = jnp.where(is_u, first, jnp.where(is_a, second, 0.0))
        coefficient = jnp.where(
            iota((1, slots), 1) < count_ref[j], weight_ref[pl.ds(j, 1), :], 0.0
        )
        onehot = jnp.where(
            iota((PANELS_DEV, slots), 0) == panel_ref[pl.ds(j, 1), :], coefficient, 0.0
        )
        wash = jnp.dot(onehot, values, precision=HIGHEST, preferred_element_type=jnp.float32)
        packed = wash[0:16]
        for g in range(1, 4):
            packed = packed + pltpu.roll(wash[16 * g : 16 * g + 16], PACK[g], 1)
        spline_out[j] = packed
        return carry

    lax.fori_loop(0, n_dom, spline_block, 0)

    def spline_copy(off):
        other = lax.rem(dom + off, n_dom)
        return pltpu.make_async_remote_copy(
            src_ref=spline_out.at[other],
            dst_ref=spline_in.at[dom],
            send_sem=spline_send.at[off],
            recv_sem=spline_recv.at[off],
            device_id=(other, case),
            device_id_type=MESH,
        )

    for off in range(1, n_dom):
        spline_copy(off).start()

    width = corners * LANES
    wide = k_ref.shape[0]
    weights = jnp.zeros((1, width), jnp.float32)
    wide_lane = iota((1, width), 1)
    for c in range(cases):
        weights = jnp.where(wide_lane % 16 == c, case_ref[c], weights)
    r = iota((width, wide), 0)
    u_dof = (r % LANES) // 16
    to_u = jnp.where(iota((width, wide), 1) == u_dof * 4 + r // LANES, 1.0, 0.0)
    q = iota((wide, width), 1)
    a_dof = ((q % LANES) // 16 + 2) % 8
    to_a = jnp.where(iota((wide, width), 0) == a_dof * 4 + q // LANES, 1.0, 0.0)
    big = jnp.dot(
        dot_lanes(to_u, k_ref[...]), to_a, precision=HIGHEST, preferred_element_type=jnp.float32
    )
    same_case = iota((width, width), 0) % 16 == iota((width, width), 1) % 16
    big = jnp.where(same_case, big * weights, 0.0)
    hi = big.astype(jnp.bfloat16)
    big_hi[...] = hi
    big_lo[...] = (big - hi.astype(jnp.float32)).astype(jnp.bfloat16)

    def unpack(side):
        base = 2 * (nodes + side * shared)
        table[pl.ds(base, shared, stride=2), :] = halo_in[side, 0:shared, :]
        both = halo_in[side, shared : shared + half, :]
        table[pl.ds(base + 1, half, stride=2), :] = jnp.where(low_half, both, 0.0)
        table[pl.ds(base + shared + 1, half, stride=2), :] = jnp.where(
            low_half, pltpu.roll(both, 64, 1), 0.0
        )

    def blank(side):
        base = 2 * (nodes + side * shared)
        table[base : base + 2 * shared, :] = jnp.zeros((2 * shared, LANES), jnp.float32)

    @pl.when(dom > 0)
    def _():
        halo_copy(1).wait_recv()
        unpack(0)

    @pl.when(dom == 0)
    def _():
        blank(0)

    @pl.when(dom < n_dom - 1)
    def _():
        halo_copy(0).wait_recv()
        unpack(1)

    @pl.when(dom == n_dom - 1)
    def _():
        blank(1)

    def pick_elements(i, carry):
        for t in range(8):
            for k in range(corners):
                e = i * 8 + t
                picked[k, pl.ds(2 * e, 2), :] = table[pl.ds(2 * conn_ref[k * elements + e], 2), :]
        return carry

    lax.fori_loop(0, elements // 8, pick_elements, 0)
    ones = jnp.ones((8, LANES), jnp.bfloat16)
    from_first = lane >= 96
    block = min(512, elements)

    def split(x):
        high = x.astype(jnp.bfloat16)
        return high, (x - high.astype(jnp.float32)).astype(jnp.bfloat16)

    def lane_sum(x):
        return lax.dot_general(
            ones, x, (((1,), (1,)), ((), ())), preferred_element_type=jnp.float32
        )

    for b in range(elements // block):
        base = 2 * b * block
        firsts = [picked[k, pl.ds(base, block, stride=2), :] for k in range(corners)]
        seconds = [picked[k, pl.ds(base + 1, block, stride=2), :] for k in range(corners)]
        u_hi, u_lo = split(jnp.concatenate(firsts, axis=1))
        force = jnp.dot(u_hi, big_hi[...], preferred_element_type=jnp.float32)
        force = force + jnp.dot(u_lo, big_hi[...], preferred_element_type=jnp.float32)
        force = force + jnp.dot(u_hi, big_lo[...], preferred_element_type=jnp.float32)
        total = jnp.zeros((block, LANES), jnp.float32)
        for k in range(corners):
            adjoint = jnp.where(from_first, firsts[k], seconds[k])
            total = total + adjoint * force[:, k * LANES : (k + 1) * LANES]
        total_hi, total_lo = split(total)
        row = (lane_sum(total_hi) + lane_sum(total_lo))[0:1]
        for part in range(block // LANES):
            at = b * (block // LANES) + part
            thick[at : at + 1, :] = row[:, part * LANES : (part + 1) * LANES]

    spline_in[dom] = spline_out[dom]
    for off in range(1, n_dom):
        spline_copy(off).wait_recv()
    wash = spline_in[0]
    for s in range(1, n_dom):
        wash = wash + spline_in[s]
    product = wash * pltpu.roll(wash, LANES - 32, 1)
    spread = jnp.concatenate(
        [
            jnp.where((lane >= PACK[g]) & (lane < PACK[g] + 16), product, 0.0)
            for g in range(4)
        ],
        axis=0,
    )
    panels = dot_lanes(jnp.broadcast_to(weights[:, 0:LANES], (8, LANES)), spread)[0:1]

    message[...] = jnp.zeros_like(message)
    for z in range(groups):
        message[z, 0:share_rows, :] = thick[z * share_rows : (z + 1) * share_rows, :]
        message[z, share_rows : share_rows + 1, 0:PANELS_DEV] = panels

    def case_copy(off):
        other = lax.rem(case + off, groups)
        return pltpu.make_async_remote_copy(
            src_ref=message.at[other],
            dst_ref=arrived.at[case],
            send_sem=case_send.at[off],
            recv_sem=case_recv.at[off],
            device_id=(dom, other),
            device_id_type=MESH,
        )

    for off in range(1, groups):
        case_copy(off).start()
    arrived[case] = message[case]
    for off in range(1, groups):
        case_copy(off).wait_recv()
    total = arrived[0]
    for z in range(1, groups):
        total = total + arrived[z]
    root = math.sqrt(cases * groups)
    scaling = scale_ref[pl.ds(case * share_rows, share_rows), :]
    thick_ref[...] = -scaling * total[0:share_rows] / root
    panel_share = PANELS_DEV // groups
    shift = lax.rem(LANES - case * panel_share, LANES)
    wash_ref[...] = pltpu.roll(total, shift, 1)[share_rows : share_rows + 1] / root

    @pl.when(dom > 0)
    def _():
        halo_copy(0).wait_send()

    @pl.when(dom < n_dom - 1)
    def _():
        halo_copy(1).wait_send()

    for off in range(1, n_dom):
        spline_copy(off).wait_send()
    for off in range(1, groups):
        case_copy(off).wait_send()


def on_device(
    n_dom,
    groups,
    displacement,
    adjoint,
    stiffness_ref,
    element_scale,
    connectivity,
    shared_nodes,
    spline_node,
    spline_panel,
    spline_weight,
    spline_count,
    case_weight,
):
    cases, dof, nodes = displacement.shape
    corners, elements = connectivity.shape
    shared = shared_nodes.shape[1]
    slots = spline_node.shape[1]
    width = corners * LANES
    share_rows = elements // LANES // groups
    packed = shared + shared // 2
    f32 = jnp.float32
    vmem = pl.BlockSpec(memory_space=pltpu.VMEM)
    hbm = pl.BlockSpec(memory_space=pltpu.HBM)
    thick, panel = pl.pallas_call(
        functools.partial(kernel, n_dom, groups),
        out_shape=(
            jax.ShapeDtypeStruct((share_rows, LANES), f32),
            jax.ShapeDtypeStruct((1, LANES), f32),
        ),
        in_specs=[hbm] * 11,
        out_specs=(vmem, vmem),
        scratch_shapes=[
            pltpu.VMEM((dof * cases, nodes), f32),
            pltpu.VMEM((dof * cases, nodes), f32),
            pltpu.VMEM(stiffness_ref.shape, f32),
            pltpu.VMEM((elements // LANES, LANES), f32),
            pltpu.VMEM(spline_panel.shape, jnp.int32),
            pltpu.VMEM(spline_weight.shape, f32),
            pltpu.SMEM((corners * elements,), jnp.int32),
            pltpu.SMEM((2 * shared,), jnp.int32),
            pltpu.SMEM((n_dom * slots,), jnp.int32),
            pltpu.SMEM(spline_count.shape, jnp.int32),
            pltpu.SMEM(case_weight.shape, f32),
            pltpu.VMEM((2 * (nodes + 2 * shared), LANES), f32),
            pltpu.VMEM((corners, 2 * elements, LANES), f32),
            pltpu.VMEM((2, 2 * shared, LANES), f32),
            pltpu.VMEM((2, packed, LANES), f32),
            pltpu.VMEM((2, packed, LANES), f32),
            pltpu.VMEM((2 * n_dom * slots, LANES), f32),
            pltpu.VMEM((n_dom, 16, LANES), f32),
            pltpu.VMEM((n_dom, 16, LANES), f32),
            pltpu.VMEM((width, width), jnp.bfloat16),
            pltpu.VMEM((width, width), jnp.bfloat16),
            pltpu.VMEM((elements // LANES, LANES), f32),
            pltpu.VMEM((groups, 8, LANES), f32),
            pltpu.VMEM((groups, 8, LANES), f32),
            pltpu.SemaphoreType.DMA((2,)),
            pltpu.SemaphoreType.DMA((2,)),
            pltpu.SemaphoreType.DMA((n_dom,)),
            pltpu.SemaphoreType.DMA((n_dom,)),
            pltpu.SemaphoreType.DMA((groups,)),
            pltpu.SemaphoreType.DMA((groups,)),
            pltpu.SemaphoreType.DMA((2, LOADS)),
            pltpu.SemaphoreType.DMA((6 + corners + 2 + n_dom,)),
        ],
        compiler_params=pltpu.CompilerParams(
            collective_id=0, has_side_effects=True, vmem_limit_bytes=62 * 2**20
        ),
    )(
        jnp.transpose(displacement, (1, 0, 2)).reshape(dof * cases, nodes),
        jnp.transpose(adjoint, (1, 0, 2)).reshape(dof * cases, nodes),
        stiffness_ref,
        element_scale.reshape(elements // LANES, LANES),
        spline_panel,
        spline_weight,
        connectivity,
        shared_nodes,
        spline_node,
        spline_count,
        case_weight,
    )
    return thick.reshape(share_rows * LANES), panel[0, : PANELS_DEV // groups]


def solution(mesh):
    return jax.shard_map(
        functools.partial(on_device, mesh.shape["dom"], mesh.shape["case"]),
        mesh=mesh,
        in_specs=(
            P("case", None, "dom"),
            P("case", None, "dom"),
            P(),
            P("dom"),
            P(None, "dom"),
            P(None, "dom"),
            P("dom", None),
            P("dom", None),
            P("dom", None),
            P("dom"),
            P("case"),
        ),
        out_specs=(P(("dom", "case")), P(("dom", "case"))),
        check_vma=False,
    )
```

```python
import functools
import math

import jax
import jax.numpy as jnp
from jax import lax
from jax.experimental import pallas as pl
from jax.experimental.pallas import tpu as pltpu
from jax.sharding import PartitionSpec as P

PANELS_DEV = 64
LANES = 128
HIGHEST = lax.Precision.HIGHEST
MESH = pl.DeviceIdType.MESH
PACK = (0, 16, 64, 80)
LOADS = 4
PARTS = 4


def iota(shape, dim):
    return lax.broadcasted_iota(jnp.int32, shape, dim)


def dot_lanes(a, b):
    return lax.dot_general(
        a, b, (((1,), (1,)), ((), ())), precision=HIGHEST, preferred_element_type=jnp.float32
    )


def kernel(
    n_dom,
    groups,
    u_hbm,
    a_hbm,
    *refs,
):
    smalls, refs = refs[:9], refs[9:]
    (thick_ref, wash_ref, u_ref, a_ref), refs = refs[:4], refs[4:]
    held, refs = refs[:9], refs[9:]
    staged, refs = dict(zip((4, 5, 6), refs[:3])), refs[3:]
    (
        k_ref,
        scale_ref,
        panel_ref,
        weight_ref,
        conn_ref,
        shared_ref,
        node_ref,
        count_ref,
        case_ref,
    ) = held
    (
        table,
        picked,
        halo_pick,
        halo_out,
        halo_in,
        spline_pick,
        spline_out,
        spline_in,
        big_hi,
        big_lo,
        thick,
        message,
        arrived,
        halo_send,
        halo_recv,
        spline_send,
        spline_recv,
        case_send,
        case_recv,
        load_sem,
        small_sem,
        index_sem,
    ) = refs
    cases = case_ref.shape[0]
    nodes = u_ref.shape[1]
    corners, elements = smalls[4].shape
    shared = smalls[5].shape[1]
    slots = smalls[6].shape[1]
    part_nodes = shared // PARTS
    half = part_nodes // 2
    share_rows = elements // LANES // groups
    dom, case = lax.axis_index("dom"), lax.axis_index("case")

    loads = []
    for part in range(LOADS):
        cols = pl.ds(part * (nodes // LOADS), nodes // LOADS)
        pair = [
            pltpu.make_async_copy(
                source.at[:, cols], target.at[:, cols], load_sem.at[which, part]
            )
            for which, (source, target) in enumerate(((u_hbm, u_ref), (a_hbm, a_ref)))
        ]
        for copy in pair:
            copy.start()
        loads.append(pair)
    small_loads = [
        pltpu.make_async_copy(source, staged.get(i, target), small_sem.at[i])
        for i, (source, target) in enumerate(zip(smalls, held))
    ]
    for copy in small_loads:
        copy.start()

    barrier = pltpu.get_barrier_semaphore()
    for off in range(1, n_dom):
        pl.semaphore_signal(
            barrier, inc=1, device_id=(lax.rem(dom + off, n_dom), case), device_id_type=MESH
        )
    for off in range(1, groups):
        pl.semaphore_signal(
            barrier, inc=1, device_id=(dom, lax.rem(case + off, groups)), device_id_type=MESH
        )

    rest = u_ref.shape[0] - 32

    def turn(block, carry):
        cols = pl.ds(pl.multiple_of(block * LANES, LANES), LANES)
        first = jnp.concatenate([u_ref[:, cols], a_ref[0:32, cols]], axis=0)
        second = jnp.concatenate(
            [a_ref[32 : 32 + rest, cols], jnp.zeros((LANES - rest, LANES), jnp.float32)], axis=0
        )
        start = pl.multiple_of(block * 2 * LANES, 2 * LANES)
        table[pl.ds(start, LANES, stride=2), :] = first.T
        table[pl.ds(start + 1, LANES, stride=2), :] = second.T
        return carry

    index_loads = []
    for i in (4, 5, 6):
        small_loads[i].wait()
        staged[i][...] = staged[i][...] * 2
        size = smalls[i].shape[1]
        for row in range(smalls[i].shape[0]):
            copy = pltpu.make_async_copy(
                staged[i].at[row],
                held[i].at[pl.ds(row * size, size)],
                index_sem.at[len(index_loads)],
            )
            copy.start()
            index_loads.append(copy)
    per_load = nodes // LANES // LOADS
    for part, pair in enumerate(loads):
        for copy in pair:
            copy.wait()
        lax.fori_loop(part * per_load, (part + 1) * per_load, turn, 0, unroll=8)
    for i, copy in enumerate(small_loads):
        if i not in staged:
            copy.wait()
    for copy in index_loads:
        copy.wait()

    lane = iota((1, LANES), 1)
    low_half = lane < 64

    def pick_halo(side, part):
        def step(i, carry):
            for t in range(16):
                n = part * part_nodes + i * 16 + t
                halo_pick[side, pl.ds(2 * n, 2), :] = table[
                    pl.ds(shared_ref[side * shared + n], 2), :
                ]
            return carry

        lax.fori_loop(0, part_nodes // 16, step, 0)
        base = 2 * part * part_nodes
        halo_out[side, part, 0:part_nodes, :] = halo_pick[
            side, pl.ds(base, part_nodes, stride=2), :
        ]
        halo_out[side, part, part_nodes : part_nodes + half, :] = halo_pick[
            side, pl.ds(base + 1, half, stride=2), :
        ] + pltpu.roll(
            halo_pick[side, pl.ds(base + part_nodes + 1, half, stride=2), :], 64, 1
        )

    def halo_copy(side, part):
        other = dom - 1 if side == 0 else dom + 1
        return pltpu.make_async_remote_copy(
            src_ref=halo_out.at[side, part],
            dst_ref=halo_in.at[1 - side, part],
            send_sem=halo_send.at[side, part],
            recv_sem=halo_recv.at[1 - side, part],
            device_id=(other, case),
            device_id_type=MESH,
        )

    for part in range(PARTS):
        pick_halo(0, part)
        if part == 0:
            pl.semaphore_wait(barrier, n_dom - 1 + groups - 1)

        @pl.when(dom > 0)
        def _():
            halo_copy(0, part).start()

        pick_halo(1, part)

        @pl.when(dom < n_dom - 1)
        def _():
            halo_copy(1, part).start()

    def pick_spline(i, carry):
        for t in range(16):
            spline_pick[pl.ds(2 * (i * 16 + t), 2), :] = table[
                pl.ds(node_ref[i * 16 + t], 2), :
            ]
        return carry

    lax.fori_loop(0, n_dom * slots // 16, pick_spline, 0)
    is_u = (lane >= 32) & (lane < 48)
    is_a = lane < 16

    def spline_block(j, carry):
        base = pl.multiple_of(j * 2 * slots, 2 * slots)
        first = spline_pick[pl.ds(base, slots, stride=2), :]
        second = spline_pick[pl.ds(base + 1, slots, stride=2), :]
        values = jnp.where(is_u, first, jnp.where(is_a, second, 0.0))
        coefficient = jnp.where(
            iota((1, slots), 1) < count_ref[j], weight_ref[pl.ds(j, 1), :], 0.0
        )
        onehot = jnp.where(
            iota((PANELS_DEV, slots), 0) == panel_ref[pl.ds(j, 1), :], coefficient, 0.0
        )
        wash = jnp.dot(onehot, values, precision=HIGHEST, preferred_element_type=jnp.float32)
        packed = wash[0:16]
        for g in range(1, 4):
            packed = packed + pltpu.roll(wash[16 * g : 16 * g + 16], PACK[g], 1)
        spline_out[j] = packed
        return carry

    lax.fori_loop(0, n_dom, spline_block, 0)

    def spline_copy(off):
        other = lax.rem(dom + off, n_dom)
        return pltpu.make_async_remote_copy(
            src_ref=spline_out.at[other],
            dst_ref=spline_in.at[dom],
            send_sem=spline_send.at[off],
            recv_sem=spline_recv.at[off],
            device_id=(other, case),
            device_id_type=MESH,
        )

    for off in range(1, n_dom):
        spline_copy(off).start()

    width = corners * LANES
    wide = k_ref.shape[0]
    weights = jnp.zeros((1, width), jnp.float32)
    wide_lane = iota((1, width), 1)
    for c in range(cases):
        weights = jnp.where(wide_lane % 16 == c, case_ref[c], weights)
    r = iota((width, wide), 0)
    u_dof = (r % LANES) // 16
    to_u = jnp.where(iota((width, wide), 1) == u_dof * 4 + r // LANES, 1.0, 0.0)
    q = iota((wide, width), 1)
    a_dof = ((q % LANES) // 16 + 2) % 8
    to_a = jnp.where(iota((wide, width), 0) == a_dof * 4 + q // LANES, 1.0, 0.0)
    big = jnp.dot(
        dot_lanes(to_u, k_ref[...]), to_a, precision=HIGHEST, preferred_element_type=jnp.float32
    )
    same_case = iota((width, width), 0) % 16 == iota((width, width), 1) % 16
    big = jnp.where(same_case, big * weights, 0.0)
    hi = big.astype(jnp.bfloat16)
    big_hi[...] = hi
    big_lo[...] = (big - hi.astype(jnp.float32)).astype(jnp.bfloat16)

    def unpack(side, part):
        base = 2 * (nodes + side * shared + part * part_nodes)
        table[pl.ds(base, part_nodes, stride=2), :] = halo_in[side, part, 0:part_nodes, :]
        both = halo_in[side, part, part_nodes : part_nodes + half, :]
        table[pl.ds(base + 1, half, stride=2), :] = jnp.where(low_half, both, 0.0)
        table[pl.ds(base + part_nodes + 1, half, stride=2), :] = jnp.where(
            low_half, pltpu.roll(both, 64, 1), 0.0
        )

    def blank(side):
        base = 2 * (nodes + side * shared)
        table[base : base + 2 * shared, :] = jnp.zeros((2 * shared, LANES), jnp.float32)

    @pl.when(dom == 0)
    def _():
        blank(0)

    @pl.when(dom == n_dom - 1)
    def _():
        blank(1)

    for part in range(PARTS):

        @pl.when(dom > 0)
        def _():
            halo_copy(1, part).wait_recv()
            unpack(0, part)

        @pl.when(dom < n_dom - 1)
        def _():
            halo_copy(0, part).wait_recv()
            unpack(1, part)

    def pick_elements(i, carry):
        for t in range(8):
            for k in range(corners):
                e = i * 8 + t
                picked[k, pl.ds(2 * e, 2), :] = table[pl.ds(conn_ref[k * elements + e], 2), :]
        return carry

    lax.fori_loop(0, elements // 8, pick_elements, 0)
    ones = jnp.ones((8, LANES), jnp.bfloat16)
    from_first = lane >= 96
    block = min(512, elements)

    def split(x):
        high = x.astype(jnp.bfloat16)
        return high, (x - high.astype(jnp.float32)).astype(jnp.bfloat16)

    def lane_sum(x):
        return lax.dot_general(
            ones, x, (((1,), (1,)), ((), ())), preferred_element_type=jnp.float32
        )

    for b in range(elements // block):
        base = 2 * b * block
        firsts = [picked[k, pl.ds(base, block, stride=2), :] for k in range(corners)]
        seconds = [picked[k, pl.ds(base + 1, block, stride=2), :] for k in range(corners)]
        u_hi, u_lo = split(jnp.concatenate(firsts, axis=1))
        force = jnp.dot(u_hi, big_hi[...], preferred_element_type=jnp.float32)
        force = force + jnp.dot(u_lo, big_hi[...], preferred_element_type=jnp.float32)
        force = force + jnp.dot(u_hi, big_lo[...], preferred_element_type=jnp.float32)
        total = jnp.zeros((block, LANES), jnp.float32)
        for k in range(corners):
            adjoint = jnp.where(from_first, firsts[k], seconds[k])
            total = total + adjoint * force[:, k * LANES : (k + 1) * LANES]
        total_hi, total_lo = split(total)
        row = (lane_sum(total_hi) + lane_sum(total_lo))[0:1]
        for part in range(block // LANES):
            at = b * (block // LANES) + part
            thick[at : at + 1, :] = row[:, part * LANES : (part + 1) * LANES]

    spline_in[dom] = spline_out[dom]
    for off in range(1, n_dom):
        spline_copy(off).wait_recv()
    wash = spline_in[0]
    for s in range(1, n_dom):
        wash = wash + spline_in[s]
    product = wash * pltpu.roll(wash, LANES - 32, 1)
    spread = jnp.concatenate(
        [
            jnp.where((lane >= PACK[g]) & (lane < PACK[g] + 16), product, 0.0)
            for g in range(4)
        ],
        axis=0,
    )
    panels = dot_lanes(jnp.broadcast_to(weights[:, 0:LANES], (8, LANES)), spread)[0:1]

    message[...] = jnp.zeros_like(message)
    for z in range(groups):
        message[z, 0:share_rows, :] = thick[z * share_rows : (z + 1) * share_rows, :]
        message[z, share_rows : share_rows + 1, 0:PANELS_DEV] = panels

    def case_copy(off):
        other = lax.rem(case + off, groups)
        return pltpu.make_async_remote_copy(
            src_ref=message.at[other],
            dst_ref=arrived.at[case],
            send_sem=case_send.at[off],
            recv_sem=case_recv.at[off],
            device_id=(dom, other),
            device_id_type=MESH,
        )

    for off in range(1, groups):
        case_copy(off).start()
    arrived[case] = message[case]
    for off in range(1, groups):
        case_copy(off).wait_recv()
    total = arrived[0]
    for z in range(1, groups):
        total = total + arrived[z]
    root = math.sqrt(cases * groups)
    scaling = scale_ref[pl.ds(case * share_rows, share_rows), :]
    thick_ref[...] = -scaling * total[0:share_rows] / root
    panel_share = PANELS_DEV // groups
    shift = lax.rem(LANES - case * panel_share, LANES)
    wash_ref[...] = pltpu.roll(total, shift, 1)[share_rows : share_rows + 1] / root

    @pl.when(dom > 0)
    def _():
        for part in range(PARTS):
            halo_copy(0, part).wait_send()

    @pl.when(dom < n_dom - 1)
    def _():
        for part in range(PARTS):
            halo_copy(1, part).wait_send()

    for off in range(1, n_dom):
        spline_copy(off).wait_send()
    for off in range(1, groups):
        case_copy(off).wait_send()


def on_device(
    n_dom,
    groups,
    displacement,
    adjoint,
    stiffness_ref,
    element_scale,
    connectivity,
    shared_nodes,
    spline_node,
    spline_panel,
    spline_weight,
    spline_count,
    case_weight,
):
    cases, dof, nodes = displacement.shape
    corners, elements = connectivity.shape
    shared = shared_nodes.shape[1]
    slots = spline_node.shape[1]
    width = corners * LANES
    share_rows = elements // LANES // groups
    packed = (shared + shared // 2) // PARTS
    f32 = jnp.float32
    vmem = pl.BlockSpec(memory_space=pltpu.VMEM)
    hbm = pl.BlockSpec(memory_space=pltpu.HBM)
    thick, panel = pl.pallas_call(
        functools.partial(kernel, n_dom, groups),
        out_shape=(
            jax.ShapeDtypeStruct((share_rows, LANES), f32),
            jax.ShapeDtypeStruct((1, LANES), f32),
        ),
        in_specs=[hbm] * 11,
        out_specs=(vmem, vmem),
        scratch_shapes=[
            pltpu.VMEM((dof * cases, nodes), f32),
            pltpu.VMEM((dof * cases, nodes), f32),
            pltpu.VMEM(stiffness_ref.shape, f32),
            pltpu.VMEM((elements // LANES, LANES), f32),
            pltpu.VMEM(spline_panel.shape, jnp.int32),
            pltpu.VMEM(spline_weight.shape, f32),
            pltpu.SMEM((corners * elements,), jnp.int32),
            pltpu.SMEM((2 * shared,), jnp.int32),
            pltpu.SMEM((n_dom * slots,), jnp.int32),
            pltpu.SMEM(spline_count.shape, jnp.int32),
            pltpu.SMEM(case_weight.shape, f32),
            pltpu.VMEM(connectivity.shape, jnp.int32),
            pltpu.VMEM(shared_nodes.shape, jnp.int32),
            pltpu.VMEM(spline_node.shape, jnp.int32),
            pltpu.VMEM((2 * (nodes + 2 * shared), LANES), f32),
            pltpu.VMEM((corners, 2 * elements, LANES), f32),
            pltpu.VMEM((2, 2 * shared, LANES), f32),
            pltpu.VMEM((2, PARTS, packed, LANES), f32),
            pltpu.VMEM((2, PARTS, packed, LANES), f32),
            pltpu.VMEM((2 * n_dom * slots, LANES), f32),
            pltpu.VMEM((n_dom, 16, LANES), f32),
            pltpu.VMEM((n_dom, 16, LANES), f32),
            pltpu.VMEM((width, width), jnp.bfloat16),
            pltpu.VMEM((width, width), jnp.bfloat16),
            pltpu.VMEM((elements // LANES, LANES), f32),
            pltpu.VMEM((groups, 8, LANES), f32),
            pltpu.VMEM((groups, 8, LANES), f32),
            pltpu.SemaphoreType.DMA((2, PARTS)),
            pltpu.SemaphoreType.DMA((2, PARTS)),
            pltpu.SemaphoreType.DMA((n_dom,)),
            pltpu.SemaphoreType.DMA((n_dom,)),
            pltpu.SemaphoreType.DMA((groups,)),
            pltpu.SemaphoreType.DMA((groups,)),
            pltpu.SemaphoreType.DMA((2, LOADS)),
            pltpu.SemaphoreType.DMA((9,)),
            pltpu.SemaphoreType.DMA((corners + 2 + n_dom,)),
        ],
        compiler_params=pltpu.CompilerParams(
            collective_id=0, has_side_effects=True, vmem_limit_bytes=62 * 2**20
        ),
    )(
        jnp.transpose(displacement, (1, 0, 2)).reshape(dof * cases, nodes),
        jnp.transpose(adjoint, (1, 0, 2)).reshape(dof * cases, nodes),
        stiffness_ref,
        element_scale.reshape(elements // LANES, LANES),
        spline_panel,
        spline_weight,
        connectivity,
        shared_nodes,
        spline_node,
        spline_count,
        case_weight,
    )
    return thick.reshape(share_rows * LANES), panel[0, : PANELS_DEV // groups]


def solution(mesh):
    return jax.shard_map(
        functools.partial(on_device, mesh.shape["dom"], mesh.shape["case"]),
        mesh=mesh,
        in_specs=(
            P("case", None, "dom"),
            P("case", None, "dom"),
            P(),
            P("dom"),
            P(None, "dom"),
            P(None, "dom"),
            P("dom", None),
            P("dom", None),
            P("dom", None),
            P("dom"),
            P("case"),
        ),
        out_specs=(P(("dom", "case")), P(("dom", "case"))),
        check_vma=False,
    )
```

```python
import functools
import math

import jax
import jax.numpy as jnp
from jax import lax
from jax.experimental import pallas as pl
from jax.experimental.pallas import tpu as pltpu
from jax.sharding import PartitionSpec as P

PANELS_DEV = 64
LANES = 128
HIGHEST = lax.Precision.HIGHEST
MESH = pl.DeviceIdType.MESH
PACK = (0, 16, 64, 80)
LOADS = 4
PARTS = 4


def iota(shape, dim):
    return lax.broadcasted_iota(jnp.int32, shape, dim)


def dot_lanes(a, b):
    return lax.dot_general(
        a, b, (((1,), (1,)), ((), ())), precision=HIGHEST, preferred_element_type=jnp.float32
    )


def kernel(
    n_dom,
    groups,
    u_hbm,
    a_hbm,
    *refs,
):
    smalls, refs = refs[:9], refs[9:]
    (out_ref, u_ref, a_ref), refs = refs[:3], refs[3:]
    held, refs = refs[:9], refs[9:]
    staged, refs = dict(zip((4, 5, 6), refs[:3])), refs[3:]
    (
        k_ref,
        scale_ref,
        panel_ref,
        weight_ref,
        conn_ref,
        shared_ref,
        node_ref,
        count_ref,
        case_ref,
    ) = held
    (
        table,
        picked,
        halo_pick,
        halo_out,
        halo_in,
        spline_pick,
        spline_out,
        spline_in,
        big_hi,
        big_lo,
        thick,
        message,
        arrived,
        halo_send,
        halo_recv,
        spline_send,
        spline_recv,
        case_send,
        case_recv,
        load_sem,
        small_sem,
        index_sem,
    ) = refs
    cases = case_ref.shape[0]
    nodes = u_ref.shape[1]
    corners, elements = smalls[4].shape
    shared = smalls[5].shape[1]
    slots = smalls[6].shape[1]
    part_nodes = shared // PARTS
    half = part_nodes // 2
    share_rows = elements // LANES // groups
    dom, case = lax.axis_index("dom"), lax.axis_index("case")

    loads = []
    for part in range(LOADS):
        cols = pl.ds(part * (nodes // LOADS), nodes // LOADS)
        pair = [
            pltpu.make_async_copy(
                source.at[:, cols], target.at[:, cols], load_sem.at[which, part]
            )
            for which, (source, target) in enumerate(((u_hbm, u_ref), (a_hbm, a_ref)))
        ]
        for copy in pair:
            copy.start()
        loads.append(pair)
    small_loads = [
        pltpu.make_async_copy(source, staged.get(i, target), small_sem.at[i])
        for i, (source, target) in enumerate(zip(smalls, held))
    ]
    for copy in small_loads:
        copy.start()

    barrier = pltpu.get_barrier_semaphore()
    for off in range(1, n_dom):
        pl.semaphore_signal(
            barrier, inc=1, device_id=(lax.rem(dom + off, n_dom), case), device_id_type=MESH
        )
    for off in range(1, groups):
        pl.semaphore_signal(
            barrier, inc=1, device_id=(dom, lax.rem(case + off, groups)), device_id_type=MESH
        )

    rest = u_ref.shape[0] - 32

    def turn(block, carry):
        cols = pl.ds(pl.multiple_of(block * LANES, LANES), LANES)
        first = jnp.concatenate([u_ref[:, cols], a_ref[0:32, cols]], axis=0)
        second = jnp.concatenate(
            [a_ref[32 : 32 + rest, cols], jnp.zeros((LANES - rest, LANES), jnp.float32)], axis=0
        )
        start = pl.multiple_of(block * 2 * LANES, 2 * LANES)
        table[pl.ds(start, LANES, stride=2), :] = first.T
        table[pl.ds(start + 1, LANES, stride=2), :] = second.T
        return carry

    index_loads = []
    for i in (4, 5, 6):
        small_loads[i].wait()
        staged[i][...] = staged[i][...] * 2
        size = smalls[i].shape[1]
        for row in range(smalls[i].shape[0]):
            copy = pltpu.make_async_copy(
                staged[i].at[row],
                held[i].at[pl.ds(row * size, size)],
                index_sem.at[len(index_loads)],
            )
            copy.start()
            index_loads.append(copy)
    per_load = nodes // LANES // LOADS
    for part, pair in enumerate(loads):
        for copy in pair:
            copy.wait()
        lax.fori_loop(part * per_load, (part + 1) * per_load, turn, 0, unroll=8)
    for i, copy in enumerate(small_loads):
        if i not in staged:
            copy.wait()
    for copy in index_loads:
        copy.wait()

    lane = iota((1, LANES), 1)
    low_half = lane < 64

    def pick_halo(side, part):
        def step(i, carry):
            for t in range(16):
                n = part * part_nodes + i * 16 + t
                halo_pick[side, pl.ds(2 * n, 2), :] = table[
                    pl.ds(shared_ref[side * shared + n], 2), :
                ]
            return carry

        lax.fori_loop(0, part_nodes // 16, step, 0)
        base = 2 * part * part_nodes
        halo_out[side, part, 0:part_nodes, :] = halo_pick[
            side, pl.ds(base, part_nodes, stride=2), :
        ]
        halo_out[side, part, part_nodes : part_nodes + half, :] = halo_pick[
            side, pl.ds(base + 1, half, stride=2), :
        ] + pltpu.roll(
            halo_pick[side, pl.ds(base + part_nodes + 1, half, stride=2), :], 64, 1
        )

    def halo_copy(side, part):
        other = dom - 1 if side == 0 else dom + 1
        return pltpu.make_async_remote_copy(
            src_ref=halo_out.at[side, part],
            dst_ref=halo_in.at[1 - side, part],
            send_sem=halo_send.at[side, part],
            recv_sem=halo_recv.at[1 - side, part],
            device_id=(other, case),
            device_id_type=MESH,
        )

    for part in range(PARTS):
        pick_halo(0, part)
        if part == 0:
            pl.semaphore_wait(barrier, n_dom - 1 + groups - 1)

        @pl.when(dom > 0)
        def _():
            halo_copy(0, part).start()

        pick_halo(1, part)

        @pl.when(dom < n_dom - 1)
        def _():
            halo_copy(1, part).start()

    def pick_spline(i, carry):
        for t in range(16):
            spline_pick[pl.ds(2 * (i * 16 + t), 2), :] = table[
                pl.ds(node_ref[i * 16 + t], 2), :
            ]
        return carry

    lax.fori_loop(0, n_dom * slots // 16, pick_spline, 0)
    is_u = (lane >= 32) & (lane < 48)
    is_a = lane < 16

    def spline_block(j, carry):
        base = pl.multiple_of(j * 2 * slots, 2 * slots)
        first = spline_pick[pl.ds(base, slots, stride=2), :]
        second = spline_pick[pl.ds(base + 1, slots, stride=2), :]
        values = jnp.where(is_u, first, jnp.where(is_a, second, 0.0))
        coefficient = jnp.where(
            iota((1, slots), 1) < count_ref[j], weight_ref[pl.ds(j, 1), :], 0.0
        )
        onehot = jnp.where(
            iota((PANELS_DEV, slots), 0) == panel_ref[pl.ds(j, 1), :], coefficient, 0.0
        )
        wash = jnp.dot(onehot, values, precision=HIGHEST, preferred_element_type=jnp.float32)
        packed = wash[0:16]
        for g in range(1, 4):
            packed = packed + pltpu.roll(wash[16 * g : 16 * g + 16], PACK[g], 1)
        spline_out[j] = packed
        return carry

    lax.fori_loop(0, n_dom, spline_block, 0)

    def spline_copy(off):
        other = lax.rem(dom + off, n_dom)
        return pltpu.make_async_remote_copy(
            src_ref=spline_out.at[other],
            dst_ref=spline_in.at[dom],
            send_sem=spline_send.at[off],
            recv_sem=spline_recv.at[off],
            device_id=(other, case),
            device_id_type=MESH,
        )

    for off in range(1, n_dom):
        spline_copy(off).start()

    width = corners * LANES
    wide = k_ref.shape[0]
    weights = jnp.zeros((1, width), jnp.float32)
    wide_lane = iota((1, width), 1)
    for c in range(cases):
        weights = jnp.where(wide_lane % 16 == c, case_ref[c], weights)
    r = iota((width, wide), 0)
    u_dof = (r % LANES) // 16
    to_u = jnp.where(iota((width, wide), 1) == u_dof * 4 + r // LANES, 1.0, 0.0)
    q = iota((wide, width), 1)
    a_dof = ((q % LANES) // 16 + 2) % 8
    to_a = jnp.where(iota((wide, width), 0) == a_dof * 4 + q // LANES, 1.0, 0.0)
    big = jnp.dot(
        dot_lanes(to_u, k_ref[...]), to_a, precision=HIGHEST, preferred_element_type=jnp.float32
    )
    same_case = iota((width, width), 0) % 16 == iota((width, width), 1) % 16
    big = jnp.where(same_case, big * weights, 0.0)
    hi = big.astype(jnp.bfloat16)
    big_hi[...] = hi
    big_lo[...] = (big - hi.astype(jnp.float32)).astype(jnp.bfloat16)

    def unpack(side, part):
        base = 2 * (nodes + side * shared + part * part_nodes)
        table[pl.ds(base, part_nodes, stride=2), :] = halo_in[side, part, 0:part_nodes, :]
        both = halo_in[side, part, part_nodes : part_nodes + half, :]
        table[pl.ds(base + 1, half, stride=2), :] = jnp.where(low_half, both, 0.0)
        table[pl.ds(base + part_nodes + 1, half, stride=2), :] = jnp.where(
            low_half, pltpu.roll(both, 64, 1), 0.0
        )

    def blank(side):
        base = 2 * (nodes + side * shared)
        table[base : base + 2 * shared, :] = jnp.zeros((2 * shared, LANES), jnp.float32)

    @pl.when(dom == 0)
    def _():
        blank(0)

    @pl.when(dom == n_dom - 1)
    def _():
        blank(1)

    for part in range(PARTS):

        @pl.when(dom > 0)
        def _():
            halo_copy(1, part).wait_recv()
            unpack(0, part)

        @pl.when(dom < n_dom - 1)
        def _():
            halo_copy(0, part).wait_recv()
            unpack(1, part)

    def pick_elements(i, carry):
        for t in range(16):
            for k in range(corners):
                e = i * 16 + t
                picked[k, pl.ds(2 * e, 2), :] = table[pl.ds(conn_ref[k * elements + e], 2), :]
        return carry

    lax.fori_loop(0, elements // 16, pick_elements, 0)
    ones = jnp.ones((8, LANES), jnp.bfloat16)
    from_first = lane >= 96
    block = min(512, elements)

    def split(x):
        high = x.astype(jnp.bfloat16)
        return high, (x - high.astype(jnp.float32)).astype(jnp.bfloat16)

    def lane_sum(x):
        return lax.dot_general(
            ones, x, (((1,), (1,)), ((), ())), preferred_element_type=jnp.float32
        )

    for b in range(elements // block):
        base = 2 * b * block
        firsts = [picked[k, pl.ds(base, block, stride=2), :] for k in range(corners)]
        seconds = [picked[k, pl.ds(base + 1, block, stride=2), :] for k in range(corners)]
        u_hi, u_lo = split(jnp.concatenate(firsts, axis=1))
        force = jnp.dot(u_hi, big_hi[...], preferred_element_type=jnp.float32)
        force = force + jnp.dot(u_lo, big_hi[...], preferred_element_type=jnp.float32)
        force = force + jnp.dot(u_hi, big_lo[...], preferred_element_type=jnp.float32)
        total = jnp.zeros((block, LANES), jnp.float32)
        for k in range(corners):
            adjoint = jnp.where(from_first, firsts[k], seconds[k])
            total = total + adjoint * force[:, k * LANES : (k + 1) * LANES]
        total_hi, total_lo = split(total)
        row = (lane_sum(total_hi) + lane_sum(total_lo))[0:1]
        for part in range(block // LANES):
            at = b * (block // LANES) + part
            thick[at : at + 1, :] = row[:, part * LANES : (part + 1) * LANES]

    spline_in[dom] = spline_out[dom]
    for off in range(1, n_dom):
        spline_copy(off).wait_recv()
    wash = spline_in[0]
    for s in range(1, n_dom):
        wash = wash + spline_in[s]
    product = wash * pltpu.roll(wash, LANES - 32, 1)
    spread = jnp.concatenate(
        [
            jnp.where((lane >= PACK[g]) & (lane < PACK[g] + 16), product, 0.0)
            for g in range(4)
        ],
        axis=0,
    )
    panels = dot_lanes(jnp.broadcast_to(weights[:, 0:LANES], (8, LANES)), spread)[0:1]

    message[...] = jnp.zeros_like(message)
    for z in range(groups):
        message[z, 0:share_rows, :] = thick[z * share_rows : (z + 1) * share_rows, :]
        message[z, share_rows : share_rows + 1, 0:PANELS_DEV] = panels

    def case_copy(off):
        other = lax.rem(case + off, groups)
        return pltpu.make_async_remote_copy(
            src_ref=message.at[other],
            dst_ref=arrived.at[case],
            send_sem=case_send.at[off],
            recv_sem=case_recv.at[off],
            device_id=(dom, other),
            device_id_type=MESH,
        )

    for off in range(1, groups):
        case_copy(off).start()
    arrived[case] = message[case]
    for off in range(1, groups):
        case_copy(off).wait_recv()
    total = arrived[0]
    for z in range(1, groups):
        total = total + arrived[z]
    root = math.sqrt(cases * groups)
    scaling = scale_ref[pl.ds(case * share_rows, share_rows), :]
    out_ref[0:share_rows, :] = -scaling * total[0:share_rows] / root
    panel_share = PANELS_DEV // groups
    shift = lax.rem(LANES - case * panel_share, LANES)
    out_ref[share_rows : share_rows + 1, :] = (
        pltpu.roll(total, shift, 1)[share_rows : share_rows + 1] / root
    )
    out_ref[share_rows + 1 : 8, :] = jnp.zeros((7 - share_rows, LANES), jnp.float32)

    @pl.when(dom > 0)
    def _():
        for part in range(PARTS):
            halo_copy(0, part).wait_send()

    @pl.when(dom < n_dom - 1)
    def _():
        for part in range(PARTS):
            halo_copy(1, part).wait_send()

    for off in range(1, n_dom):
        spline_copy(off).wait_send()
    for off in range(1, groups):
        case_copy(off).wait_send()


def on_device(
    n_dom,
    groups,
    displacement,
    adjoint,
    stiffness_ref,
    element_scale,
    connectivity,
    shared_nodes,
    spline_node,
    spline_panel,
    spline_weight,
    spline_count,
    case_weight,
):
    cases, dof, nodes = displacement.shape
    corners, elements = connectivity.shape
    shared = shared_nodes.shape[1]
    slots = spline_node.shape[1]
    width = corners * LANES
    share_rows = elements // LANES // groups
    packed = (shared + shared // 2) // PARTS
    f32 = jnp.float32
    vmem = pl.BlockSpec(memory_space=pltpu.VMEM)
    hbm = pl.BlockSpec(memory_space=pltpu.HBM)
    out = pl.pallas_call(
        functools.partial(kernel, n_dom, groups),
        out_shape=jax.ShapeDtypeStruct((8, LANES), f32),
        in_specs=[hbm] * 11,
        out_specs=vmem,
        scratch_shapes=[
            pltpu.VMEM((dof * cases, nodes), f32),
            pltpu.VMEM((dof * cases, nodes), f32),
            pltpu.VMEM(stiffness_ref.shape, f32),
            pltpu.VMEM((elements // LANES, LANES), f32),
            pltpu.VMEM(spline_panel.shape, jnp.int32),
            pltpu.VMEM(spline_weight.shape, f32),
            pltpu.SMEM((corners * elements,), jnp.int32),
            pltpu.SMEM((2 * shared,), jnp.int32),
            pltpu.SMEM((n_dom * slots,), jnp.int32),
            pltpu.SMEM(spline_count.shape, jnp.int32),
            pltpu.SMEM(case_weight.shape, f32),
            pltpu.VMEM(connectivity.shape, jnp.int32),
            pltpu.VMEM(shared_nodes.shape, jnp.int32),
            pltpu.VMEM(spline_node.shape, jnp.int32),
            pltpu.VMEM((2 * (nodes + 2 * shared), LANES), f32),
            pltpu.VMEM((corners, 2 * elements, LANES), f32),
            pltpu.VMEM((2, 2 * shared, LANES), f32),
            pltpu.VMEM((2, PARTS, packed, LANES), f32),
            pltpu.VMEM((2, PARTS, packed, LANES), f32),
            pltpu.VMEM((2 * n_dom * slots, LANES), f32),
            pltpu.VMEM((n_dom, 16, LANES), f32),
            pltpu.VMEM((n_dom, 16, LANES), f32),
            pltpu.VMEM((width, width), jnp.bfloat16),
            pltpu.VMEM((width, width), jnp.bfloat16),
            pltpu.VMEM((elements // LANES, LANES), f32),
            pltpu.VMEM((groups, 8, LANES), f32),
            pltpu.VMEM((groups, 8, LANES), f32),
            pltpu.SemaphoreType.DMA((2, PARTS)),
            pltpu.SemaphoreType.DMA((2, PARTS)),
            pltpu.SemaphoreType.DMA((n_dom,)),
            pltpu.SemaphoreType.DMA((n_dom,)),
            pltpu.SemaphoreType.DMA((groups,)),
            pltpu.SemaphoreType.DMA((groups,)),
            pltpu.SemaphoreType.DMA((2, LOADS)),
            pltpu.SemaphoreType.DMA((9,)),
            pltpu.SemaphoreType.DMA((corners + 2 + n_dom,)),
        ],
        compiler_params=pltpu.CompilerParams(
            collective_id=0, has_side_effects=True, vmem_limit_bytes=62 * 2**20
        ),
    )(
        jnp.transpose(displacement, (1, 0, 2)).reshape(dof * cases, nodes),
        jnp.transpose(adjoint, (1, 0, 2)).reshape(dof * cases, nodes),
        stiffness_ref,
        element_scale.reshape(elements // LANES, LANES),
        spline_panel,
        spline_weight,
        connectivity,
        shared_nodes,
        spline_node,
        spline_count,
        case_weight,
    )
    return (
        out[:share_rows].reshape(share_rows * LANES),
        out[share_rows, : PANELS_DEV // groups],
    )


def solution(mesh):
    return jax.shard_map(
        functools.partial(on_device, mesh.shape["dom"], mesh.shape["case"]),
        mesh=mesh,
        in_specs=(
            P("case", None, "dom"),
            P("case", None, "dom"),
            P(),
            P("dom"),
            P(None, "dom"),
            P(None, "dom"),
            P("dom", None),
            P("dom", None),
            P("dom", None),
            P("dom"),
            P("case"),
        ),
        out_specs=(P(("dom", "case")), P(("dom", "case"))),
        check_vma=False,
    )
```
